256 devices in a mesh: row: 8 (over x_lo, y), col: 16 (over z, x_hi), pole: 2 (over core).
Axes of the slice: x: 4 (x_hi: 2, x_lo: 2; x = x_hi * 2 + x_lo), y: 4, z: 8, core: 2. Of those that a mesh axis runs over, the one named last changes fastest.
Arguments:
- ainv: bfloat16 [2, 2, 10240, 10240], P('pole', None, 'row', 'col'), may hold values from -0.0625 to 0.0625
- pattern: int32 [80, 80], P('row', 'col'), may hold values from 0 to 1, as said below
- rows_a: int32 [80], P('col'), may hold values 0 or 1
- rows_b: int32 [80], P('col'), may hold values 0 or 1
- panel_a: bfloat16 [2, 2, 256, 10240], P('pole', None, 'row', 'col'), may hold values from -6 to 6
- panel_b: bfloat16 [2, 2, 256, 10240], P('pole', None, 'row', 'col'), may hold values from -6 to 6
- tri_inv_a: bfloat16 [2, 2, 256, 256], P('pole'), may hold values from -0.375 to 0.375
- tri_inv_b: bfloat16 [2, 2, 256, 256], P('pole'), may hold values from -0.375 to 0.375
- cross_b: bfloat16 [2, 2, 256, 256], P('pole'), may hold values from -0.375 to 0.375
- weights: float32 [2, 2], P('pole'), may hold values from -4 to 4
Outputs:
- dens_a: float32 [10240, 256], P(('row', 'col'), 'pole')
- dens_b: float32 [10240, 256], P(('row', 'col'), 'pole')
The draws below stay inside these ranges and needn't reach their ends.
Inputs may be any that keep to these rules, and one draw needn't show every extreme that they name: 1 marks a selected block of the ancestor inverse, 0 a block outside the pattern; the share of selected blocks differs between block rows. `rows_a`: 1 marks an ancestor block row in the first supernode's structure. `rows_b`: 1 marks an ancestor block row in the second supernode's structure.
All inputs are finite; a program needn't handle non-finite values.
Results may differ from the reference program's by a relative error of at most 0.02.
Values may be sent and summed in bfloat16 or wider, within the bound.
A program may use at most 64 MiB of HBM per device.

```python
import jax
import jax.numpy as jnp
from jax import lax

W = 256
R = 10240
BS = 128
NB = 80
POLES = 2
N_COL = 16


def draw_pattern(key, part):
    block_row = jnp.arange(NB, dtype=jnp.int32)[:, None]
    threshold = 2 + 5 * block_row // max(NB - 1, 1)
    values = jax.random.randint(key, (NB, NB), 0, 8)
    return (values < threshold).astype(jnp.int32)


def with_ends(result, own_key, least, largest):
    dims = result.shape
    index_at = [jax.random.randint(jax.random.fold_in(own_key, axis), (), 0, dims[axis]) for axis in range(len(dims))]
    result = result.at[tuple(index_at)].set(least)
    longest = dims.index(max(dims))
    index_at[longest] = (index_at[longest] + 1) % dims[longest]
    return result.at[tuple(index_at)].set(largest)


def level_of(rng, shape, pieces, least, top_value):
    def one(position, shards_of):
        heights = jax.random.uniform(jax.random.fold_in(jax.random.fold_in(rng, 6), position), (shards_of,), jnp.float32, least / len(pieces), top_value / len(pieces))
        return jnp.repeat(jnp.exp(heights), shape[position] // shards_of).reshape((-1,) + (1,) * (len(shape) - position - 1))

    level = one(*pieces[0])
    for cut in pieces[1:]:
        level = level * one(*cut)
    return level


def bell_draw(rng, dims, scale, most, shards=(), held_as=jnp.bfloat16):
    result = jax.random.normal(rng, dims, jnp.float32) * scale
    if len(shards) > 0:
        result = level_of(rng, dims, shards, -0.22, 0.18) * result
    return jnp.clip(result, min=-most, max=most).astype(held_as)


def setup_inputs(seed: int = 0) -> dict:
    seeds = jax.random.split(jax.random.key(seed), 11)
    return {
        "ainv": bell_draw(seeds[0], (POLES, 2, R, R), R ** -0.5, 0.0625, ((0, 2), (2, 8), (3, 16))),
        "pattern": draw_pattern(jax.random.fold_in(seeds[10], 71), 0),
        "rows_a": with_ends((jax.random.randint(seeds[2], (NB,), 0, 4) < 3).astype(jnp.int32), jax.random.fold_in(seeds[2], 1), 0, 1),
        "rows_b": with_ends((jax.random.randint(seeds[3], (NB,), 0, 4) < 3).astype(jnp.int32), jax.random.fold_in(seeds[3], 1), 0, 1),
        "panel_a": bell_draw(seeds[4], (POLES, 2, W, R), 1.0, 6.0, ((0, 2), (2, 8), (3, 16))),
        "panel_b": bell_draw(seeds[5], (POLES, 2, W, R), 1.0, 6.0, ((0, 2), (2, 8), (3, 16))),
        "tri_inv_a": bell_draw(seeds[6], (POLES, 2, W, W), W ** -0.5, 0.375, ((0, 2),)),
        "tri_inv_b": bell_draw(seeds[7], (POLES, 2, W, W), W ** -0.5, 0.375, ((0, 2),)),
        "cross_b": bell_draw(seeds[8], (POLES, 2, W, W), W ** -0.5, 0.375, ((0, 2),)),
        "weights": bell_draw(seeds[9], (POLES, 2), 1.0, 4.0, ((0, 2),), jnp.float32),
    }


def complex_product(left, right, precision_mode=None):
    real_part = jnp.dot(left[0], right[0], preferred_element_type=jnp.float32, precision=precision_mode) - jnp.dot(left[1], right[1], preferred_element_type=jnp.float32, precision=precision_mode)
    imag_part = jnp.dot(left[0], right[1], preferred_element_type=jnp.float32, precision=precision_mode) + jnp.dot(left[1], right[0], preferred_element_type=jnp.float32, precision=precision_mode)
    return jnp.stack([real_part, imag_part])


def scaled_panel(panel, rows, tri):
    keep_mask = jnp.repeat(rows, BS).astype(jnp.bfloat16)
    lower_rows = jnp.transpose(panel, (0, 2, 1)) * keep_mask[None, :, None]
    return complex_product(lower_rows, tri).astype(jnp.bfloat16)


def reference(ainv, pattern, rows_a, rows_b, panel_a, panel_b, tri_inv_a, tri_inv_b, cross_b, weights):
    col_width = R // N_COL
    col_blocks = col_width // BS
    dens_a = jnp.zeros((R, W), jnp.float32)
    dens_b = jnp.zeros((R, W), jnp.float32)
    for pole_index in range(POLES):
        lhat_a = scaled_panel(panel_a[pole_index], rows_a, tri_inv_a[pole_index])
        lhat_b = scaled_panel(panel_b[pole_index], rows_b, tri_inv_b[pole_index])
        cross_hat = complex_product(cross_b[pole_index], tri_inv_b[pole_index]).astype(jnp.bfloat16)
        matrix = ainv[pole_index]

        def add_block(carry, block_index):
            begin = (block_index * col_width).astype(jnp.int32)
            columns = lax.dynamic_slice_in_dim(matrix, begin, col_width, 2)
            marks = lax.dynamic_slice_in_dim(pattern, (block_index * col_blocks).astype(jnp.int32), col_blocks, 1)
            spread = jnp.repeat(jnp.repeat(marks, BS, 0), BS, 1).astype(jnp.bfloat16)
            columns = columns * spread[None]
            term_a = complex_product(columns, lax.dynamic_slice_in_dim(lhat_a, begin, col_width, 1))
            term_b = complex_product(columns, lax.dynamic_slice_in_dim(lhat_b, begin, col_width, 1))
            term_a = lax.optimization_barrier(term_a.astype(jnp.bfloat16)).astype(jnp.float32)
            term_b = lax.optimization_barrier(term_b.astype(jnp.bfloat16)).astype(jnp.float32)
            return (carry[0] + term_a, carry[1] + term_b), None

        zeros = jnp.zeros((2, R, W), jnp.float32)
        (sum_a, sum_b), unused = lax.scan(add_block, (zeros, zeros), jnp.arange(N_COL, dtype=jnp.int32))
        update_a = -sum_a
        update_b = -sum_b - complex_product(update_a, cross_hat.astype(jnp.float32), lax.Precision.HIGHEST)
        w_real = weights[pole_index, 0]
        w_imag = weights[pole_index, 1]
        dens_a = dens_a + w_real * update_a[1] + w_imag * update_a[0]
        dens_b = dens_b + w_real * update_b[1] + w_imag * update_b[0]
    return dens_a, dens_b
```

```python
import functools

import jax
import jax.numpy as jnp
from jax import lax
from jax.experimental import pallas as pl
from jax.experimental.pallas import tpu as pltpu
from jax.sharding import PartitionSpec as P

BS = 128
CHUNKS = 4
MESH = pl.DeviceIdType.MESH
NT = (((1,), (1,)), ((), ()))


def remote(src, dst, send, recv, where):
    return pltpu.make_async_remote_copy(
        src_ref=src,
        dst_ref=dst,
        send_sem=send,
        recv_sem=recv,
        device_id=where,
        device_id_type=MESH,
    )


def lane_marks(marks, count):
    return jnp.concatenate(
        [jnp.full((1, BS), marks(j), jnp.int32) for j in range(count)], axis=1
    ).astype(jnp.float32).astype(jnp.bfloat16)


def kernel(
    nrow,
    ncol,
    ainv,
    pattern,
    rows_a,
    rows_b,
    panel_a,
    panel_b,
    tri_a,
    tri_b,
    cross,
    weights,
    out_a,
    out_b,
    a_cat,
    pan,
    full,
    mt,
    xt,
    gt,
    part,
    fromp,
    total,
    rs,
    a_sem,
    pan_sem,
    g_send,
    g_recv,
    p_send,
    p_recv,
    r_send,
    r_recv,
):
    me_r, me_c, me_p = (lax.axis_index(name) for name in ("row", "col", "pole"))
    other = 1 - me_p
    tile_rows, tile_cols = ainv.shape[2], ainv.shape[3]
    width = tri_a.shape[2]
    share = tile_rows // ncol
    chunk = tile_rows // CHUNKS
    per_chunk = ncol // CHUNKS
    panels, marks, outs = (panel_a, panel_b), (rows_a, rows_b), (out_a, out_b)

    pan_copies = [
        pltpu.make_async_copy(panels[s].at[0], pan.at[s], pan_sem.at[s]) for s in range(2)
    ]
    a_copies = [
        pltpu.make_async_copy(
            ainv.at[0, d], a_cat.at[:, d * tile_cols : (d + 1) * tile_cols], a_sem.at[d]
        )
        for d in range(2)
    ]
    for copy in pan_copies + a_copies:
        copy.start()

    barrier = pltpu.get_barrier_semaphore()

    def greet(name, index, size):
        @pl.loop(1, size)
        def _(i):
            pl.semaphore_signal(
                barrier,
                inc=1,
                device_id={name: lax.rem(index + i, size)},
                device_id_type=MESH,
            )

    greet("row", me_r, nrow)
    greet("col", me_c, ncol)
    pl.semaphore_signal(barrier, inc=1, device_id={"pole": other}, device_id_type=MESH)

    for s in range(2):
        pan_copies[s].wait()
        keep = lane_marks(lambda j: marks[s][j], tile_cols // BS)
        full[s, me_r] = pan[s] * keep[None]

    pl.semaphore_wait(barrier, nrow + ncol - 1)

    def gather_copy(s, i):
        return remote(
            full.at[s, me_r],
            full.at[s, me_r],
            g_send.at[s, i],
            g_recv.at[s, i],
            {"row": lax.rem(me_r + i, nrow)},
        )

    for s in range(2):

        @pl.loop(1, nrow)
        def _(i):
            gather_copy(s, i).start()

    w_re, w_im = weights[0, 0], weights[0, 1]
    for s, tri in enumerate((tri_a, tri_b)):
        t_re, t_im = tri[0, 0].astype(jnp.float32), tri[0, 1].astype(jnp.float32)
        m_re = (w_im * t_im - w_re * t_re).T.astype(jnp.bfloat16)
        m_im = (-w_im * t_re - w_re * t_im).T.astype(jnp.bfloat16)
        mt[s, :width, :width] = m_im
        mt[s, :width, width:] = m_re
        mt[s, width:, :width] = m_re
        mt[s, width:, width:] = -m_im

    def mul(a, b):
        return jnp.dot(a, b, preferred_element_type=jnp.float32)

    x_re = (mul(cross[0, 0], tri_b[0, 0]) - mul(cross[0, 1], tri_b[0, 1])).T.astype(jnp.bfloat16)
    x_im = (mul(cross[0, 0], tri_b[0, 1]) + mul(cross[0, 1], tri_b[0, 0])).T.astype(jnp.bfloat16)
    xt[:width, :width] = -x_re
    xt[:width, width:] = -x_im
    xt[width:, :width] = x_im
    xt[width:, width:] = -x_re

    for copy in a_copies:
        copy.wait()

    @pl.loop(0, tile_rows // BS)
    def _(b):
        rows = pl.ds(pl.multiple_of(b * BS, BS), BS)
        keep = lane_marks(lambda j: pattern[j, b], tile_cols // BS)
        for d in range(2):
            columns = slice(d * tile_cols, (d + 1) * tile_cols)
            a_cat[rows, columns] = a_cat[rows, columns] * keep

    def pole_copy(s, q):
        rows = pl.ds(pl.multiple_of(q * chunk, chunk), chunk)
        return remote(
            part.at[s, other, rows],
            fromp.at[s, rows],
            p_send.at[s, q],
            p_recv.at[s, q],
            {"pole": other},
        )

    def sum_copy(s, i):
        to = lax.rem(me_c + i, ncol)
        return remote(
            total.at[s, to], rs.at[s, me_c], r_send.at[s, i], r_recv.at[s, i], {"col": to}
        )

    for s in range(2):

        @pl.loop(1, nrow)
        def _(i):
            gather_copy(s, i).wait_recv()

        for half in range(2):
            o_rows = slice(half * width, (half + 1) * width)
            lower = [full[s, :, d].reshape(width, tile_cols) for d in range(2)]
            g = mul(mt[s, o_rows, :width], lower[0]) + mul(mt[s, o_rows, width:], lower[1])
            if s == 1:
                g += mul(xt[o_rows, :width], gt[0, :, :tile_cols])
                g += mul(xt[o_rows, width:], gt[0, :, tile_cols:])
            gt[s, :, half * tile_cols : (half + 1) * tile_cols] = g.astype(jnp.bfloat16)

        first = lax.div(me_c, per_chunk)

        @pl.loop(0, CHUNKS)
        def _(n):
            q = lax.rem(first + 1 + n, CHUNKS)
            rows = pl.ds(pl.multiple_of(q * chunk, chunk), chunk)
            c = lax.dot_general(a_cat[rows, :], gt[s], NT, preferred_element_type=jnp.float32)
            c = c.astype(jnp.bfloat16)
            part[s, 0, rows] = c[:, :BS]
            part[s, 1, rows] = c[:, BS:]
            pole_copy(s, q).start()

        @pl.loop(0, CHUNKS)
        def _(n):
            q = lax.rem(first + 1 + n, CHUNKS)
            rows = pl.ds(pl.multiple_of(q * chunk, chunk), chunk)
            pole_copy(s, q).wait_recv()
            both = part[s, me_p, rows].astype(jnp.float32) + fromp[s, rows].astype(jnp.float32)
            total[s, pl.ds(q * per_chunk, per_chunk)] = both.astype(jnp.bfloat16).reshape(
                per_chunk, share, BS
            )

        @pl.loop(1, ncol)
        def _(i):
            sum_copy(s, i).start()

    for s in range(2):

        def add(i, acc):
            sum_copy(s, i).wait_recv()
            frm = lax.rem(me_c - i + ncol, ncol)
            return acc + rs[s, frm].astype(jnp.float32)

        outs[s][...] = lax.fori_loop(1, ncol, add, total[s, me_c].astype(jnp.float32))

    for s in range(2):

        @pl.loop(1, nrow)
        def _(i):
            gather_copy(s, i).wait_send()

        @pl.loop(0, CHUNKS)
        def _(q):
            pole_copy(s, q).wait_send()

        @pl.loop(1, ncol)
        def _(i):
            sum_copy(s, i).wait_send()


def solution(mesh):
    nrow, ncol = mesh.shape["row"], mesh.shape["col"]

    def per_device(
        ainv, pattern, rows_a, rows_b, panel_a, panel_b, tri_a, tri_b, cross_b, weights
    ):
        tile_rows, tile_cols = ainv.shape[2:]
        width, own_width = tri_a.shape[2], panel_a.shape[2]
        share = tile_rows // ncol
        anywhere = pl.BlockSpec(memory_space=pl.ANY)
        scalars = pl.BlockSpec(memory_space=pltpu.SMEM)
        whole = pl.BlockSpec(memory_space=pltpu.VMEM)
        bf16 = jnp.bfloat16
        dma = pltpu.SemaphoreType.DMA
        return pl.pallas_call(
            functools.partial(kernel, nrow, ncol),
            out_shape=[jax.ShapeDtypeStruct((share, BS), jnp.float32)] * 2,
            in_specs=[anywhere]
            + [scalars] * 3
            + [anywhere] * 2
            + [whole] * 3
            + [scalars],
            out_specs=[whole] * 2,
            scratch_shapes=[
                pltpu.VMEM((tile_rows, 2 * tile_cols), bf16),
                pltpu.VMEM((2, 2, own_width, tile_cols), bf16),
                pltpu.VMEM((2, nrow, 2, own_width, tile_cols), bf16),
                pltpu.VMEM((2, 2 * width, 2 * width), bf16),
                pltpu.VMEM((2 * width, 2 * width), bf16),
                pltpu.VMEM((2, width, 2 * tile_cols), bf16),
                pltpu.VMEM((2, 2, tile_rows, BS), bf16),
                pltpu.VMEM((2, tile_rows, BS), bf16),
                pltpu.VMEM((2, ncol, share, BS), bf16),
                pltpu.VMEM((2, ncol, share, BS), bf16),
                dma((2,)),
                dma((2,)),
                dma((2, nrow)),
                dma((2, nrow)),
                dma((2, CHUNKS)),
                dma((2, CHUNKS)),
                dma((2, ncol)),
                dma((2, ncol)),
            ],
            compiler_params=pltpu.CompilerParams(
                collective_id=0, has_side_effects=True, vmem_limit_bytes=56 << 20
            ),
        )(ainv, pattern.T, rows_a, rows_b, panel_a, panel_b, tri_a, tri_b, cross_b, weights)

    placed = (
        P("pole", None, "row", "col"),
        P("row", "col"),
        P("col"),
        P("col"),
        P("pole", None, "row", "col"),
        P("pole", None, "row", "col"),
        P("pole", None, None, None),
        P("pole", None, None, None),
        P("pole", None, None, None),
        P("pole", None),
    )
    return jax.shard_map(
        per_device,
        mesh=mesh,
        in_specs=placed,
        out_specs=(P(("row", "col"), "pole"), P(("row", "col"), "pole")),
        check_vma=False,
    )
```

```python
import functools

import jax
import jax.numpy as jnp
from jax import lax
from jax.experimental import pallas as pl
from jax.experimental.pallas import tpu as pltpu
from jax.sharding import PartitionSpec as P

BS = 128
CHUNKS = 4
LAG = 3
LATE = 1
MESH = pl.DeviceIdType.MESH
NT = (((1,), (1,)), ((), ()))


def remote(src, dst, send, recv, where):
    return pltpu.make_async_remote_copy(
        src_ref=src,
        dst_ref=dst,
        send_sem=send,
        recv_sem=recv,
        device_id=where,
        device_id_type=MESH,
    )


def lane_marks(marks, count):
    return jnp.concatenate(
        [jnp.full((1, BS), marks(j), jnp.int32) for j in range(count)], axis=1
    ).astype(jnp.float32).astype(jnp.bfloat16)


def spread(out, a_ref, b_ref):
    a_ref[...] = out[0]
    b_ref[...] = out[1]


def kernel(
    nrow,
    ncol,
    ainv,
    pattern,
    rows_a,
    rows_b,
    panel_a,
    panel_b,
    tri_a,
    tri_b,
    cross,
    weights,
    out,
    a_cat,
    pan,
    tri,
    full,
    mt,
    xt,
    gt,
    part,
    fromp,
    total,
    fromx,
    summed,
    rs,
    a_sem,
    pan_sem,
    tri_sem,
    g_send,
    g_recv,
    p_send,
    p_recv,
    x_send,
    x_recv,
    r_send,
    r_recv,
):
    me_r, me_c, me_p = (lax.axis_index(name) for name in ("row", "col", "pole"))
    other = 1 - me_p
    tile_rows, tile_cols = ainv.shape[2], ainv.shape[3]
    width = tri_a.shape[2]
    share = tile_rows // ncol
    chunk = tile_rows // CHUNKS
    per_chunk = ncol // CHUNKS
    ring = nrow // 2
    nz = ncol // 2
    me_z, me_h = lax.div(me_c, 2), lax.rem(me_c, 2)
    per_z = nz // CHUNKS

    def col_at(z, h):
        return z * 2 + h

    marks = (rows_a, rows_b)

    pan_copies = [
        pltpu.make_async_copy(ref.at[0], pan.at[s], pan_sem.at[s])
        for s, ref in enumerate((panel_a, panel_b))
    ]
    tri_copies = [
        pltpu.make_async_copy(ref.at[0], tri.at[s], tri_sem.at[s])
        for s, ref in enumerate((tri_a, tri_b, cross))
    ]
    a_copies = [
        pltpu.make_async_copy(
            ainv.at[0, d], a_cat.at[:, d * tile_cols : (d + 1) * tile_cols], a_sem.at[d]
        )
        for d in range(2)
    ]
    for copy in pan_copies:
        copy.start()

    def row_at(step):
        dx, dy = step
        x, y = lax.div(me_r, ring), lax.rem(me_r, ring)
        return lax.rem(x + dx, 2) * ring + lax.rem(y + dy + ring, ring)

    barrier = pltpu.get_barrier_semaphore()
    row_partners = ((0, 1), (0, -1), (0, 2), (1, 0))
    for step in row_partners:
        pl.semaphore_signal(
            barrier, inc=1, device_id={"row": row_at(step)}, device_id_type=MESH
        )
    pl.semaphore_signal(barrier, inc=1, device_id={"pole": other}, device_id_type=MESH)

    pl.semaphore_signal(
        barrier, inc=1, device_id={"col": col_at(me_z, 1 - me_h)}, device_id_type=MESH
    )

    @pl.loop(1, nz)
    def _(i):
        pl.semaphore_signal(
            barrier,
            inc=1,
            device_id={"col": col_at(lax.rem(me_z + i, nz), me_h)},
            device_id_type=MESH,
        )

    for copy in tri_copies + a_copies:
        copy.start()

    for s in range(2):
        pan_copies[s].wait()
        keep = lane_marks(lambda j: marks[s][j], tile_cols // BS)
        full[s, me_r] = pan[s] * keep[None]

    pl.semaphore_wait(barrier, len(row_partners) + nz + 1)

    hops = (
        ((0, 2), (0, 0), None),
        ((0, 1), (0, 0), None),
        ((0, -1), (0, 0), None),
        ((1, 0), (0, 0), None),
        ((0, 1), (1, 0), 3),
        ((0, -1), (1, 0), 3),
        ((1, 0), (0, 2), 0),
    )

    def gather_copy(s, i):
        to, owner, _ = hops[i]
        block = full.at[s, row_at(owner)]
        return remote(block, block, g_send.at[s, i], g_recv.at[s, i], {"row": row_at(to)})

    for s in range(2):
        for i in range(4):
            gather_copy(s, i).start()

    w_re, w_im = weights[0, 0], weights[0, 1]

    def scale(s):
        tri_copies[s].wait()
        t_re, t_im = tri[s, 0].astype(jnp.float32), tri[s, 1].astype(jnp.float32)
        m_re = (w_im * t_im - w_re * t_re).T.astype(jnp.bfloat16)
        m_im = (-w_im * t_re - w_re * t_im).T.astype(jnp.bfloat16)
        mt[s, :width, :width] = m_im
        mt[s, :width, width:] = m_re
        mt[s, width:, :width] = m_re
        mt[s, width:, width:] = -m_im

    scale(0)

    for s in range(2):
        gather_copy(s, 3).wait_recv()
        gather_copy(s, 4).start()
        gather_copy(s, 5).start()
        gather_copy(s, 0).wait_recv()
        gather_copy(s, 6).start()

    for copy in a_copies:
        copy.wait()

    @pl.loop(0, tile_rows // BS)
    def _(b):
        rows = pl.ds(pl.multiple_of(b * BS, BS), BS)
        keep = lane_marks(lambda j: pattern[j, b], tile_cols // BS)
        for d in range(2):
            columns = slice(d * tile_cols, (d + 1) * tile_cols)
            a_cat[rows, columns] = a_cat[rows, columns] * keep

    def mul(a, b):
        return jnp.dot(a, b, preferred_element_type=jnp.float32)

    def couple():
        tri_copies[2].wait()
        x_re = mul(tri[2, 0], tri[1, 0]) - mul(tri[2, 1], tri[1, 1])
        x_im = mul(tri[2, 0], tri[1, 1]) + mul(tri[2, 1], tri[1, 0])
        x_re, x_im = x_re.T.astype(jnp.bfloat16), x_im.T.astype(jnp.bfloat16)
        xt[:width, :width] = -x_re
        xt[:width, width:] = -x_im
        xt[width:, :width] = x_im
        xt[width:, width:] = -x_re

    scale(1)
    couple()

    def pole_copy(s, q):
        rows = pl.ds(pl.multiple_of(q * chunk, chunk), chunk)
        return remote(
            part.at[s, other, rows],
            fromp.at[s, rows],
            p_send.at[s, q],
            p_recv.at[s, q],
            {"pole": other},
        )

    def x_copy(s, q):
        shares = pl.ds(q * per_z, per_z)
        return remote(
            total.at[s, 1 - me_h, shares],
            fromx.at[s, shares],
            x_send.at[s, q],
            x_recv.at[s, q],
            {"col": col_at(me_z, 1 - me_h)},
        )

    def send_copy(s, to):
        return remote(
            summed.at[s, to],
            rs.at[s, me_z],
            r_send.at[s, to],
            r_recv.at[s, me_z],
            {"col": col_at(to, me_h)},
        )

    def take_copy(s, frm):
        return remote(
            summed.at[s, me_z],
            rs.at[s, frm],
            r_send.at[s, me_z],
            r_recv.at[s, frm],
            {"col": col_at(frm, me_h)},
        )

    first = lax.div(me_c, per_chunk)

    def turn(n):
        off = jnp.where(n == 0, 2, jnp.where(n == 1, 1, jnp.where(n == 2, 3, 0)))
        return lax.rem(first + off, CHUNKS)

    def pass_on(s):
        @pl.loop(0, CHUNKS)
        def _(n):
            q = turn(n)
            x_copy(s, q).wait_recv()
            shares = pl.ds(q * per_z, per_z)
            summed[s, shares] = (
                total[s, me_h, shares].astype(jnp.float32) + fromx[s, shares].astype(jnp.float32)
            ).astype(jnp.bfloat16)
            for j in range(per_z):
                to = q * per_z + j

                @pl.when(to != me_z)
                def _():
                    send_copy(s, to).start()

    for s in range(2):
        for i in (1, 2, 4, 5, 6):
            gather_copy(s, i).wait_recv()

        for half in range(2):
            o_rows = slice(half * width, (half + 1) * width)
            lower = [full[s, :, d].reshape(width, tile_cols) for d in range(2)]
            g = mul(mt[s, o_rows, :width], lower[0]) + mul(mt[s, o_rows, width:], lower[1])
            if s == 1:
                g += mul(xt[o_rows, :width], gt[0, :, :tile_cols])
                g += mul(xt[o_rows, width:], gt[0, :, tile_cols:])
            gt[s, :, half * tile_cols : (half + 1) * tile_cols] = g.astype(jnp.bfloat16)

        @pl.loop(0, CHUNKS + LAG)
        def _(n):
            @pl.when(n < CHUNKS)
            def _():
                q = turn(n)
                rows = pl.ds(pl.multiple_of(q * chunk, chunk), chunk)
                c = lax.dot_general(
                    a_cat[rows, :], gt[s], NT, preferred_element_type=jnp.float32
                ).astype(jnp.bfloat16)
                part[s, 0, rows] = c[:, :BS]
                part[s, 1, rows] = c[:, BS:]
                pole_copy(s, q).start()

            @pl.when(n >= LAG)
            def _():
                q = turn(n - LAG)
                rows = pl.ds(pl.multiple_of(q * chunk, chunk), chunk)
                pole_copy(s, q).wait_recv()
                both = part[s, me_p, rows].astype(jnp.float32) + fromp[s, rows].astype(jnp.float32)
                both = both.astype(jnp.bfloat16).reshape(per_z, 2, share, BS)
                for h in range(2):
                    for j in range(per_z):
                        total[s, h, q * per_z + j] = both[j, h]
                x_copy(s, q).start()

        if s >= LATE:
            for late in range(s - LATE, s + 1 if s == 1 else s - LATE + 1):
                pass_on(late)

    for s in range(2):

        def add(i, acc):
            frm = lax.rem(me_z + i, nz)
            take_copy(s, frm).wait_recv()
            return acc + rs[s, frm].astype(jnp.float32)

        out[s] = lax.fori_loop(1, nz, add, summed[s, me_z].astype(jnp.float32))

    for s in range(2):
        for i in range(len(hops)):
            gather_copy(s, i).wait_send()

        @pl.loop(0, CHUNKS)
        def _(q):
            pole_copy(s, q).wait_send()
            x_copy(s, q).wait_send()

        @pl.loop(1, nz)
        def _(i):
            send_copy(s, lax.rem(me_z + i, nz)).wait_send()


def solution(mesh):
    nrow, ncol = mesh.shape["row"], mesh.shape["col"]

    def per_device(
        ainv, pattern, rows_a, rows_b, panel_a, panel_b, tri_a, tri_b, cross_b, weights
    ):
        tile_rows, tile_cols = ainv.shape[2:]
        width, own_width = tri_a.shape[2], panel_a.shape[2]
        share = tile_rows // ncol
        anywhere = pl.BlockSpec(memory_space=pl.ANY)
        scalars = pl.BlockSpec(memory_space=pltpu.SMEM)
        whole = pl.BlockSpec(memory_space=pltpu.VMEM)
        bf16 = jnp.bfloat16
        dma = pltpu.SemaphoreType.DMA
        dens = pl.pallas_call(
            functools.partial(kernel, nrow, ncol),
            out_shape=jax.ShapeDtypeStruct((2, share, BS), jnp.float32),
            in_specs=[anywhere] + [scalars] * 3 + [anywhere] * 5 + [scalars],
            out_specs=whole,
            scratch_shapes=[
                pltpu.VMEM((tile_rows, 2 * tile_cols), bf16),
                pltpu.VMEM((2, 2, own_width, tile_cols), bf16),
                pltpu.VMEM((3, 2, width, width), bf16),
                pltpu.VMEM((2, nrow, 2, own_width, tile_cols), bf16),
                pltpu.VMEM((2, 2 * width, 2 * width), bf16),
                pltpu.VMEM((2 * width, 2 * width), bf16),
                pltpu.VMEM((2, width, 2 * tile_cols), bf16),
                pltpu.VMEM((2, 2, tile_rows, BS), bf16),
                pltpu.VMEM((2, tile_rows, BS), bf16),
                pltpu.VMEM((2, 2, ncol // 2, share, BS), bf16),
                pltpu.VMEM((2, ncol // 2, share, BS), bf16),
                pltpu.VMEM((2, ncol // 2, share, BS), bf16),
                pltpu.VMEM((2, ncol // 2, share, BS), bf16),
                dma((2,)),
                dma((2,)),
                dma((3,)),
                dma((2, 7)),
                dma((2, 7)),
                dma((2, CHUNKS)),
                dma((2, CHUNKS)),
                dma((2, CHUNKS)),
                dma((2, CHUNKS)),
                dma((2, ncol // 2)),
                dma((2, ncol // 2)),
            ],
            compiler_params=pltpu.CompilerParams(
                collective_id=0, has_side_effects=True, vmem_limit_bytes=56 << 20
            ),
        )(ainv, pattern.T, rows_a, rows_b, panel_a, panel_b, tri_a, tri_b, cross_b, weights)
        return pl.pallas_call(
            spread,
            out_shape=[jax.ShapeDtypeStruct((share, BS), jnp.float32)] * 2,
            in_specs=[whole],
            out_specs=[whole] * 2,
        )(dens)

    placed = (
        P("pole", None, "row", "col"),
        P("row", "col"),
        P("col"),
        P("col"),
        P("pole", None, "row", "col"),
        P("pole", None, "row", "col"),
        P("pole", None, None, None),
        P("pole", None, None, None),
        P("pole", None, None, None),
        P("pole", None),
    )
    return jax.shard_map(
        per_device,
        mesh=mesh,
        in_specs=placed,
        out_specs=(P(("row", "col"), "pole"), P(("row", "col"), "pole")),
        check_vma=False,
    )
```

```python
import functools

import jax
import jax.numpy as jnp
from jax import lax
from jax.experimental import pallas as pl
from jax.experimental.pallas import tpu as pltpu
from jax.sharding import PartitionSpec as P

BS = 128
CHUNKS = 4
MESH = pl.DeviceIdType.MESH
NT = (((1,), (1,)), ((), ()))


def remote(src, dst, send, recv, where):
    return pltpu.make_async_remote_copy(
        src_ref=src,
        dst_ref=dst,
        send_sem=send,
        recv_sem=recv,
        device_id=where,
        device_id_type=MESH,
    )


def lane_marks(marks, count):
    return jnp.concatenate(
        [jnp.full((1, BS), marks(j), jnp.int32) for j in range(count)], axis=1
    ).astype(jnp.float32).astype(jnp.bfloat16)


def spread(out, a_ref, b_ref):
    a_ref[...] = out[0]
    b_ref[...] = out[1]


def kernel(
    nrow,
    ncol,
    ainv,
    pattern,
    rows_a,
    rows_b,
    panel_a,
    panel_b,
    tri_a,
    tri_b,
    cross,
    weights,
    out,
    a_cat,
    pan,
    tri,
    full,
    mt,
    xt,
    gt,
    coupled,
    part,
    fromp,
    total,
    fromx,
    summed,
    rs,
    a_sem,
    pan_sem,
    tri_sem,
    g_send,
    g_recv,
    p_send,
    p_recv,
    x_send,
    x_recv,
    r_send,
    r_recv,
    in_sem,
):
    me_r, me_c, me_p = (lax.axis_index(name) for name in ("row", "col", "pole"))
    other = 1 - me_p
    tile_rows, tile_cols = ainv.shape[2], ainv.shape[3]
    width = tri_a.shape[2]
    share = tile_rows // ncol
    chunk = tile_rows // CHUNKS
    per_chunk = ncol // CHUNKS
    ring = nrow // 2
    nz = ncol // 2
    me_z, me_h = lax.div(me_c, 2), lax.rem(me_c, 2)
    per_z = nz // CHUNKS

    def col_at(z, h):
        return z * 2 + h

    marks = (rows_a, rows_b)

    pan_copies = [
        pltpu.make_async_copy(ref.at[0], pan.at[s], pan_sem.at[s])
        for s, ref in enumerate((panel_a, panel_b))
    ]
    tri_copies = [
        pltpu.make_async_copy(ref.at[0], tri.at[s], tri_sem.at[s])
        for s, ref in enumerate((tri_a, tri_b, cross))
    ]
    a_copies = [
        pltpu.make_async_copy(
            ainv.at[0, d], a_cat.at[:, d * tile_cols : (d + 1) * tile_cols], a_sem.at[d]
        )
        for d in range(2)
    ]
    for copy in pan_copies:
        copy.start()

    def row_at(step):
        dx, dy = step
        x, y = lax.div(me_r, ring), lax.rem(me_r, ring)
        return lax.rem(x + dx, 2) * ring + lax.rem(y + dy + ring, ring)

    barrier = pltpu.get_barrier_semaphore()
    row_partners = ((0, 1), (0, -1), (0, 2), (1, 0))
    for step in row_partners:
        pl.semaphore_signal(
            barrier, inc=1, device_id={"row": row_at(step)}, device_id_type=MESH
        )
    pl.semaphore_signal(barrier, inc=1, device_id={"pole": other}, device_id_type=MESH)

    pl.semaphore_signal(
        barrier, inc=1, device_id={"col": col_at(me_z, 1 - me_h)}, device_id_type=MESH
    )

    def along_z(step):
        return {"col": col_at(lax.rem(me_z + step + nz, nz), me_h)}

    for step in (1, -1):
        pl.semaphore_signal(barrier, inc=1, device_id=along_z(step), device_id_type=MESH)

    for copy in tri_copies + a_copies:
        copy.start()

    for s in range(2):
        pan_copies[s].wait()
        keep = lane_marks(lambda j: marks[s][j], tile_cols // BS)
        full[s, me_r] = pan[s] * keep[None]

    pl.semaphore_wait(barrier, len(row_partners) + 4)

    hops = ((((1,0),(0,0),None,None),((0,2),(0,0),None,None),((0,1),(0,0),None,None),((0,-1),(0,0),None,None),((0,1),(1,0),None,0),((0,-1),(1,0),None,0),((1,0),(0,2),None,1)), (((1,0),(0,0),None,None),((0,2),(0,0),None,None),((0,1),(0,0),None,None),((0,-1),(0,0),None,None),((0,1),(1,0),None,0),((0,-1),(1,0),None,0),((1,0),(0,2),None,1)))

    def gather_copy(s, i):
        to, owner, part_of, _ = hops[s][i]
        block = full.at[s, row_at(owner)]
        if part_of is not None:
            block = block.at[part_of]
        return remote(block, block, g_send.at[s, i], g_recv.at[s, i], {"row": row_at(to)})

    arrived = set()

    def arrive(s, i):
        if (s, i) not in arrived:
            arrived.add((s, i))
            gather_copy(s, i).wait_recv()

    def pass_blocks(order):
        for s, i in order:
            if hops[s][i][3] is not None:
                arrive(s, hops[s][i][3])
            gather_copy(s, i).start()

    def tell(turn_of):
        for side, step in enumerate((1, -1)):
            pl.semaphore_signal(
                in_sem.at[turn_of, side],
                inc=1,
                device_id=along_z(step * (turn_of + 1)),
                device_id_type=MESH,
            )

    def hear(turn_of):
        for side in range(2):
            pl.semaphore_wait(in_sem.at[turn_of, side], 1)

    tell(0)
    pass_blocks(((0, 0), (0, 1), (1, 0), (1, 1), (0, 2), (0, 3), (1, 2), (1, 3)))

    w_re, w_im = weights[0, 0], weights[0, 1]

    def scale(s):
        tri_copies[s].wait()
        t_re, t_im = tri[s, 0].astype(jnp.float32), tri[s, 1].astype(jnp.float32)
        m_re = (w_im * t_im - w_re * t_re).T.astype(jnp.bfloat16)
        m_im = (-w_im * t_re - w_re * t_im).T.astype(jnp.bfloat16)
        mt[s, :width, :width] = m_im
        mt[s, :width, width:] = m_re
        mt[s, width:, :width] = m_re
        mt[s, width:, width:] = -m_im

    hear(0)
    tell(1)
    scale(0)

    pass_blocks(((0, 4), (0, 5), (0, 6), (1, 4), (1, 5), (1, 6)))

    for copy in a_copies:
        copy.wait()

    @pl.loop(0, tile_rows // BS)
    def _(b):
        rows = pl.ds(pl.multiple_of(b * BS, BS), BS)
        keep = lane_marks(lambda j: pattern[j, b], tile_cols // BS)
        for d in range(2):
            columns = slice(d * tile_cols, (d + 1) * tile_cols)
            a_cat[rows, columns] = a_cat[rows, columns] * keep

    def mul(a, b):
        return jnp.dot(a, b, preferred_element_type=jnp.float32)

    def couple():
        tri_copies[2].wait()
        x_re = mul(tri[2, 0], tri[1, 0]) - mul(tri[2, 1], tri[1, 1])
        x_im = mul(tri[2, 0], tri[1, 1]) + mul(tri[2, 1], tri[1, 0])
        x_re, x_im = x_re.T.astype(jnp.bfloat16), x_im.T.astype(jnp.bfloat16)
        xt[:width, :width] = -x_re
        xt[:width, width:] = -x_im
        xt[width:, :width] = x_im
        xt[width:, width:] = -x_re

    scale(1)
    couple()
    hear(1)

    def pole_copy(s, q):
        rows = pl.ds(pl.multiple_of(q * chunk, chunk), chunk)
        return remote(
            part.at[s, other, rows],
            fromp.at[s, rows],
            p_send.at[s, q],
            p_recv.at[s, q],
            {"pole": other},
        )

    def x_copy(s, q):
        shares = pl.ds(q * per_z, per_z)
        return remote(
            total.at[s, 1 - me_h, shares],
            fromx.at[s, shares],
            x_send.at[s, q],
            x_recv.at[s, q],
            {"col": col_at(me_z, 1 - me_h)},
        )

    def send_copy(s, to):
        return remote(
            summed.at[s, to],
            rs.at[s, me_z],
            r_send.at[s, to],
            r_recv.at[s, me_z],
            {"col": col_at(to, me_h)},
        )

    def take_copy(s, frm):
        return remote(
            summed.at[s, me_z],
            rs.at[s, frm],
            r_send.at[s, me_z],
            r_recv.at[s, frm],
            {"col": col_at(frm, me_h)},
        )

    first = lax.div(me_c, per_chunk)

    def turn(n):
        off = CHUNKS // 2 + lax.div(n + 1, 2) * (1 - 2 * lax.rem(n, 2))
        return lax.rem(first + off, CHUNKS)

    def pass_on(s):
        @pl.loop(0, CHUNKS)
        def _(n):
            q = turn(n)
            x_copy(s, q).wait_recv()
            shares = pl.ds(q * per_z, per_z)
            summed[s, shares] = (
                total[s, me_h, shares].astype(jnp.float32) + fromx[s, shares].astype(jnp.float32)
            ).astype(jnp.bfloat16)
            for j in range(per_z):
                to = q * per_z + j

                @pl.when(to != me_z)
                def _():
                    send_copy(s, to).start()

    for s in range(2):
        for i in range(len(hops[s])):
            arrive(s, i)

        for half in range(2):
            o_rows = slice(half * width, (half + 1) * width)
            lower = [full[s, :, d].reshape(width, tile_cols) for d in range(2)]
            g = mul(mt[s, o_rows, :width], lower[0]) + mul(mt[s, o_rows, width:], lower[1])
            if s == 1:
                g += coupled[half]
            gt[s, :, half * tile_cols : (half + 1) * tile_cols] = g.astype(jnp.bfloat16)

        @pl.loop(0, CHUNKS)
        def _(n):
            q = turn(n)
            rows = pl.ds(pl.multiple_of(q * chunk, chunk), chunk)
            c = lax.dot_general(
                a_cat[rows, :], gt[s], NT, preferred_element_type=jnp.float32
            ).astype(jnp.bfloat16)
            part[s, 0, rows] = c[:, :BS]
            part[s, 1, rows] = c[:, BS:]
            pole_copy(s, q).start()

        if s == 0:
            for half in range(2):
                o_rows = slice(half * width, (half + 1) * width)
                coupled[half] = mul(xt[o_rows, :width], gt[0, :, :tile_cols]) + mul(
                    xt[o_rows, width:], gt[0, :, tile_cols:]
                )

        @pl.loop(0, CHUNKS)
        def _(n):
            q = turn(n)
            rows = pl.ds(pl.multiple_of(q * chunk, chunk), chunk)
            pole_copy(s, q).wait_recv()
            both = part[s, me_p, rows].astype(jnp.float32) + fromp[s, rows].astype(jnp.float32)
            both = both.astype(jnp.bfloat16).reshape(per_z, 2, share, BS)
            for h in range(2):
                for j in range(per_z):
                    total[s, h, q * per_z + j] = both[j, h]
            x_copy(s, q).start()

    for s in range(2):
        pass_on(s)

    for s in range(2):

        def add(i, acc):
            frm = lax.rem(me_z + i, nz)
            take_copy(s, frm).wait_recv()
            return acc + rs[s, frm].astype(jnp.float32)

        out[s] = lax.fori_loop(1, nz, add, summed[s, me_z].astype(jnp.float32))

    for s in range(2):
        for i in range(len(hops[s])):
            gather_copy(s, i).wait_send()

        @pl.loop(0, CHUNKS)
        def _(q):
            pole_copy(s, q).wait_send()
            x_copy(s, q).wait_send()

        @pl.loop(1, nz)
        def _(i):
            send_copy(s, lax.rem(me_z + i, nz)).wait_send()


def solution(mesh):
    nrow, ncol = mesh.shape["row"], mesh.shape["col"]

    def per_device(
        ainv, pattern, rows_a, rows_b, panel_a, panel_b, tri_a, tri_b, cross_b, weights
    ):
        tile_rows, tile_cols = ainv.shape[2:]
        width, own_width = tri_a.shape[2], panel_a.shape[2]
        share = tile_rows // ncol
        anywhere = pl.BlockSpec(memory_space=pl.ANY)
        scalars = pl.BlockSpec(memory_space=pltpu.SMEM)
        whole = pl.BlockSpec(memory_space=pltpu.VMEM)
        bf16 = jnp.bfloat16
        dma = pltpu.SemaphoreType.DMA
        dens = pl.pallas_call(
            functools.partial(kernel, nrow, ncol),
            out_shape=jax.ShapeDtypeStruct((2, share, BS), jnp.float32),
            in_specs=[anywhere] + [scalars] * 3 + [anywhere] * 5 + [scalars],
            out_specs=whole,
            scratch_shapes=[
                pltpu.VMEM((tile_rows, 2 * tile_cols), bf16),
                pltpu.VMEM((2, 2, own_width, tile_cols), bf16),
                pltpu.VMEM((3, 2, width, width), bf16),
                pltpu.VMEM((2, nrow, 2, own_width, tile_cols), bf16),
                pltpu.VMEM((2, 2 * width, 2 * width), bf16),
                pltpu.VMEM((2 * width, 2 * width), bf16),
                pltpu.VMEM((2, width, 2 * tile_cols), bf16),
                pltpu.VMEM((2, width, tile_cols), jnp.float32),
                pltpu.VMEM((2, 2, tile_rows, BS), bf16),
                pltpu.VMEM((2, tile_rows, BS), bf16),
                pltpu.VMEM((2, 2, ncol // 2, share, BS), bf16),
                pltpu.VMEM((2, ncol // 2, share, BS), bf16),
                pltpu.VMEM((2, ncol // 2, share, BS), bf16),
                pltpu.VMEM((2, ncol // 2, share, BS), bf16),
                dma((2,)),
                dma((2,)),
                dma((3,)),
                dma((2, 10)),
                dma((2, 10)),
                dma((2, CHUNKS)),
                dma((2, CHUNKS)),
                dma((2, CHUNKS)),
                dma((2, CHUNKS)),
                dma((2, ncol // 2)),
                dma((2, ncol // 2)),
                pltpu.SemaphoreType.REGULAR((2, 2)),
            ],
            compiler_params=pltpu.CompilerParams(
                collective_id=0, has_side_effects=True, vmem_limit_bytes=56 << 20
            ),
        )(ainv, pattern.T, rows_a, rows_b, panel_a, panel_b, tri_a, tri_b, cross_b, weights)
        return pl.pallas_call(
            spread,
            out_shape=[jax.ShapeDtypeStruct((share, BS), jnp.float32)] * 2,
            in_specs=[whole],
            out_specs=[whole] * 2,
        )(dens)

    placed = (
        P("pole", None, "row", "col"),
        P("row", "col"),
        P("col"),
        P("col"),
        P("pole", None, "row", "col"),
        P("pole", None, "row", "col"),
        P("pole", None, None, None),
        P("pole", None, None, None),
        P("pole", None, None, None),
        P("pole", None),
    )
    return jax.shard_map(
        per_device,
        mesh=mesh,
        in_specs=placed,
        out_specs=(P(("row", "col"), "pole"), P(("row", "col"), "pole")),
        check_vma=False,
    )
```

```python
import functools

import jax
import jax.numpy as jnp
from jax import lax
from jax.experimental import pallas as pl
from jax.experimental.pallas import tpu as pltpu
from jax.sharding import PartitionSpec as P

BS = 128
CHUNKS = 4
MESH = pl.DeviceIdType.MESH
NT = (((1,), (1,)), ((), ()))


def remote(src, dst, send, recv, where):
    return pltpu.make_async_remote_copy(
        src_ref=src,
        dst_ref=dst,
        send_sem=send,
        recv_sem=recv,
        device_id=where,
        device_id_type=MESH,
    )


def lane_marks(marks, count):
    return jnp.concatenate(
        [jnp.full((1, BS), marks(j), jnp.int32) for j in range(count)], axis=1
    ).astype(jnp.float32).astype(jnp.bfloat16)


def kernel(
    nrow,
    ncol,
    ainv,
    pattern,
    rows_a,
    rows_b,
    panel_a,
    panel_b,
    tri_a,
    tri_b,
    cross,
    weights,
    out,
    a_cat,
    pan,
    tri,
    full,
    mt,
    xt,
    gt,
    coupled,
    part,
    fromp,
    total,
    fromx,
    summed,
    rs,
    a_sem,
    pan_sem,
    tri_sem,
    g_send,
    g_recv,
    p_send,
    p_recv,
    x_send,
    x_recv,
    r_send,
    r_recv,
    in_sem,
):
    me_r, me_c, me_p = (lax.axis_index(name) for name in ("row", "col", "pole"))
    other = 1 - me_p
    tile_rows, tile_cols = ainv.shape[2], ainv.shape[3]
    width = tri_a.shape[2]
    share = tile_rows // ncol
    chunk = tile_rows // CHUNKS
    per_chunk = ncol // CHUNKS
    ring = nrow // 2
    nz = ncol // 2
    me_z, me_h = lax.div(me_c, 2), lax.rem(me_c, 2)
    per_z = nz // CHUNKS

    def col_at(z, h):
        return z * 2 + h

    marks = (rows_a, rows_b)

    pan_copies = [
        pltpu.make_async_copy(ref.at[0], pan.at[s], pan_sem.at[s])
        for s, ref in enumerate((panel_a, panel_b))
    ]
    tri_copies = [
        pltpu.make_async_copy(ref.at[0], tri.at[s], tri_sem.at[s])
        for s, ref in enumerate((tri_a, tri_b, cross))
    ]
    a_copies = [
        pltpu.make_async_copy(
            ainv.at[0, d], a_cat.at[:, d * tile_cols : (d + 1) * tile_cols], a_sem.at[d]
        )
        for d in range(2)
    ]
    for copy in pan_copies:
        copy.start()

    def row_at(step):
        dx, dy = step
        x, y = lax.div(me_r, ring), lax.rem(me_r, ring)
        return lax.rem(x + dx, 2) * ring + lax.rem(y + dy + ring, ring)

    barrier = pltpu.get_barrier_semaphore()
    row_partners = ((0, 1), (0, -1), (0, 2), (1, 0))
    for step in row_partners:
        pl.semaphore_signal(
            barrier, inc=1, device_id={"row": row_at(step)}, device_id_type=MESH
        )
    pl.semaphore_signal(barrier, inc=1, device_id={"pole": other}, device_id_type=MESH)

    pl.semaphore_signal(
        barrier, inc=1, device_id={"col": col_at(me_z, 1 - me_h)}, device_id_type=MESH
    )

    def along_z(step):
        return {"col": col_at(lax.rem(me_z + step + nz, nz), me_h)}

    for step in (1, -1):
        pl.semaphore_signal(barrier, inc=1, device_id=along_z(step), device_id_type=MESH)

    for copy in tri_copies + a_copies:
        copy.start()

    for s in range(2):
        pan_copies[s].wait()
        keep = lane_marks(lambda j: marks[s][j], tile_cols // BS)
        full[s, me_r] = pan[s] * keep[None]

    pl.semaphore_wait(barrier, len(row_partners) + 4)

    hops = ((((1,0),(0,0),None,None),((0,2),(0,0),None,None),((0,1),(0,0),None,None),((0,-1),(0,0),None,None),((0,1),(1,0),None,0),((0,-1),(1,0),None,0),((1,0),(0,2),None,1)), (((1,0),(0,0),None,None),((0,2),(0,0),None,None),((0,1),(0,0),None,None),((0,-1),(0,0),None,None),((0,1),(1,0),None,0),((0,-1),(1,0),None,0),((1,0),(0,2),None,1)))

    def gather_copy(s, i):
        to, owner, part_of, _ = hops[s][i]
        block = full.at[s, row_at(owner)]
        if part_of is not None:
            block = block.at[part_of]
        return remote(block, block, g_send.at[s, i], g_recv.at[s, i], {"row": row_at(to)})

    arrived = set()

    def arrive(s, i):
        if (s, i) not in arrived:
            arrived.add((s, i))
            gather_copy(s, i).wait_recv()

    def pass_blocks(order):
        for s, i in order:
            if hops[s][i][3] is not None:
                arrive(s, hops[s][i][3])
            gather_copy(s, i).start()

    def tell(turn_of):
        for side, step in enumerate((1, -1)):
            pl.semaphore_signal(
                in_sem.at[turn_of, side],
                inc=1,
                device_id=along_z(step * (turn_of + 1)),
                device_id_type=MESH,
            )

    def hear(turn_of):
        for side in range(2):
            pl.semaphore_wait(in_sem.at[turn_of, side], 1)

    tell(0)
    pass_blocks(((0, 0), (0, 1), (1, 0), (1, 1), (0, 2), (0, 3), (1, 2), (1, 3)))

    w_re, w_im = weights[0, 0], weights[0, 1]

    def scale(s):
        tri_copies[s].wait()
        t_re, t_im = tri[s, 0].astype(jnp.float32), tri[s, 1].astype(jnp.float32)
        m_re = (w_im * t_im - w_re * t_re).T.astype(jnp.bfloat16)
        m_im = (-w_im * t_re - w_re * t_im).T.astype(jnp.bfloat16)
        mt[s, :width, :width] = m_im
        mt[s, :width, width:] = m_re
        mt[s, width:, :width] = m_re
        mt[s, width:, width:] = -m_im

    hear(0)
    tell(1)
    scale(0)

    pass_blocks(((0, 4), (0, 5), (0, 6), (1, 4), (1, 5), (1, 6)))

    for copy in a_copies:
        copy.wait()

    @pl.loop(0, tile_rows // BS)
    def _(b):
        rows = pl.ds(pl.multiple_of(b * BS, BS), BS)
        keep = lane_marks(lambda j: pattern[j, b], tile_cols // BS)
        for d in range(2):
            columns = slice(d * tile_cols, (d + 1) * tile_cols)
            a_cat[rows, columns] = a_cat[rows, columns] * keep

    def mul(a, b):
        return jnp.dot(a, b, preferred_element_type=jnp.float32)

    def couple():
        tri_copies[2].wait()
        x_re = mul(tri[2, 0], tri[1, 0]) - mul(tri[2, 1], tri[1, 1])
        x_im = mul(tri[2, 0], tri[1, 1]) + mul(tri[2, 1], tri[1, 0])
        x_re, x_im = x_re.T.astype(jnp.bfloat16), x_im.T.astype(jnp.bfloat16)
        xt[:width, :width] = -x_re
        xt[:width, width:] = -x_im
        xt[width:, :width] = x_im
        xt[width:, width:] = -x_re

    scale(1)
    couple()
    hear(1)

    def pole_copy(s, q):
        rows = pl.ds(pl.multiple_of(q * chunk, chunk), chunk)
        return remote(
            part.at[s, other, rows],
            fromp.at[s, rows],
            p_send.at[s, q],
            p_recv.at[s, q],
            {"pole": other},
        )

    def x_copy(s, q):
        shares = pl.ds(q * per_z, per_z)
        return remote(
            total.at[s, 1 - me_h, shares],
            fromx.at[s, shares],
            x_send.at[s, q],
            x_recv.at[s, q],
            {"col": col_at(me_z, 1 - me_h)},
        )

    def send_copy(s, to):
        return remote(
            summed.at[s, to],
            rs.at[s, me_z],
            r_send.at[s, to],
            r_recv.at[s, me_z],
            {"col": col_at(to, me_h)},
        )

    def take_copy(s, frm):
        return remote(
            summed.at[s, me_z],
            rs.at[s, frm],
            r_send.at[s, me_z],
            r_recv.at[s, frm],
            {"col": col_at(frm, me_h)},
        )

    first = lax.div(me_c, per_chunk)

    def turn(n):
        off = CHUNKS // 2 + lax.div(n + 1, 2) * (1 - 2 * lax.rem(n, 2))
        return lax.rem(first + off, CHUNKS)

    def pass_on(s):
        @pl.loop(0, CHUNKS)
        def _(n):
            q = turn(n)
            x_copy(s, q).wait_recv()
            shares = pl.ds(q * per_z, per_z)
            summed[s, shares] = (
                total[s, me_h, shares].astype(jnp.float32) + fromx[s, shares].astype(jnp.float32)
            ).astype(jnp.bfloat16)
            for j in range(per_z):
                to = q * per_z + j

                @pl.when(to != me_z)
                def _():
                    send_copy(s, to).start()

    for s in range(2):
        for i in range(len(hops[s])):
            arrive(s, i)

        for half in range(2):
            o_rows = slice(half * width, (half + 1) * width)
            lower = [full[s, :, d].reshape(width, tile_cols) for d in range(2)]
            g = mul(mt[s, o_rows, :width], lower[0]) + mul(mt[s, o_rows, width:], lower[1])
            if s == 1:
                g += coupled[half]
            gt[s, :, half * tile_cols : (half + 1) * tile_cols] = g.astype(jnp.bfloat16)

        @pl.loop(0, CHUNKS)
        def _(n):
            q = turn(n)
            rows = pl.ds(pl.multiple_of(q * chunk, chunk), chunk)
            c = lax.dot_general(
                a_cat[rows, :], gt[s], NT, preferred_element_type=jnp.float32
            ).astype(jnp.bfloat16)
            part[s, 0, rows] = c[:, :BS]
            part[s, 1, rows] = c[:, BS:]
            pole_copy(s, q).start()

        if s == 0:
            for half in range(2):
                o_rows = slice(half * width, (half + 1) * width)
                coupled[half] = mul(xt[o_rows, :width], gt[0, :, :tile_cols]) + mul(
                    xt[o_rows, width:], gt[0, :, tile_cols:]
                )

        @pl.loop(0, CHUNKS)
        def _(n):
            q = turn(n)
            rows = pl.ds(pl.multiple_of(q * chunk, chunk), chunk)
            pole_copy(s, q).wait_recv()
            both = part[s, me_p, rows].astype(jnp.float32) + fromp[s, rows].astype(jnp.float32)
            both = both.astype(jnp.bfloat16).reshape(per_z, 2, share, BS)
            for h in range(2):
                for j in range(per_z):
                    total[s, h, q * per_z + j] = both[j, h]
            x_copy(s, q).start()

    for s in range(2):
        pass_on(s)

    for s in range(2):
        for i in range(len(hops[s])):
            gather_copy(s, i).wait_send()

        @pl.loop(0, CHUNKS)
        def _(q):
            pole_copy(s, q).wait_send()
            x_copy(s, q).wait_send()

    for s in range(2):

        def add(i, acc):
            frm = lax.rem(me_z + i, nz)
            take_copy(s, frm).wait_recv()
            return acc + rs[s, frm].astype(jnp.float32)

        out[s] = lax.fori_loop(1, nz, add, summed[s, me_z].astype(jnp.float32))

    for s in range(2):

        @pl.loop(1, nz)
        def _(i):
            send_copy(s, lax.rem(me_z + i, nz)).wait_send()


def solution(mesh):
    nrow, ncol = mesh.shape["row"], mesh.shape["col"]

    def per_device(
        ainv, pattern, rows_a, rows_b, panel_a, panel_b, tri_a, tri_b, cross_b, weights
    ):
        tile_rows, tile_cols = ainv.shape[2:]
        width, own_width = tri_a.shape[2], panel_a.shape[2]
        share = tile_rows // ncol
        anywhere = pl.BlockSpec(memory_space=pl.ANY)
        scalars = pl.BlockSpec(memory_space=pltpu.SMEM)
        whole = pl.BlockSpec(memory_space=pltpu.VMEM)
        bf16 = jnp.bfloat16
        dma = pltpu.SemaphoreType.DMA
        dens = pl.pallas_call(
            functools.partial(kernel, nrow, ncol),
            out_shape=pltpu.VMEM((2, share, BS), jnp.float32),
            in_specs=[anywhere] + [scalars] * 3 + [anywhere] * 5 + [scalars],
            out_specs=whole,
            scratch_shapes=[
                pltpu.VMEM((tile_rows, 2 * tile_cols), bf16),
                pltpu.VMEM((2, 2, own_width, tile_cols), bf16),
                pltpu.VMEM((3, 2, width, width), bf16),
                pltpu.VMEM((2, nrow, 2, own_width, tile_cols), bf16),
                pltpu.VMEM((2, 2 * width, 2 * width), bf16),
                pltpu.VMEM((2 * width, 2 * width), bf16),
                pltpu.VMEM((2, width, 2 * tile_cols), bf16),
                pltpu.VMEM((2, width, tile_cols), jnp.float32),
                pltpu.VMEM((2, 2, tile_rows, BS), bf16),
                pltpu.VMEM((2, tile_rows, BS), bf16),
                pltpu.VMEM((2, 2, ncol // 2, share, BS), bf16),
                pltpu.VMEM((2, ncol // 2, share, BS), bf16),
                pltpu.VMEM((2, ncol // 2, share, BS), bf16),
                pltpu.VMEM((2, ncol // 2, share, BS), bf16),
                dma((2,)),
                dma((2,)),
                dma((3,)),
                dma((2, 10)),
                dma((2, 10)),
                dma((2, CHUNKS)),
                dma((2, CHUNKS)),
                dma((2, CHUNKS)),
                dma((2, CHUNKS)),
                dma((2, ncol // 2)),
                dma((2, ncol // 2)),
                pltpu.SemaphoreType.REGULAR((2, 2)),
            ],
            compiler_params=pltpu.CompilerParams(
                collective_id=0, has_side_effects=True, vmem_limit_bytes=56 << 20
            ),
        )(ainv, pattern.T, rows_a, rows_b, panel_a, panel_b, tri_a, tri_b, cross_b, weights)
        return dens[0], dens[1]

    placed = (
        P("pole", None, "row", "col"),
        P("row", "col"),
        P("col"),
        P("col"),
        P("pole", None, "row", "col"),
        P("pole", None, "row", "col"),
        P("pole", None, None, None),
        P("pole", None, None, None),
        P("pole", None, None, None),
        P("pole", None),
    )
    return jax.shard_map(
        per_device,
        mesh=mesh,
        in_specs=placed,
        out_specs=(P(("row", "col"), "pole"), P(("row", "col"), "pole")),
        check_vma=False,
    )
```

```python
import functools

import jax
import jax.numpy as jnp
from jax import lax
from jax.experimental import pallas as pl
from jax.experimental.pallas import tpu as pltpu
from jax.sharding import PartitionSpec as P

BS = 128
CHUNKS = 4
MESH = pl.DeviceIdType.MESH
NT = (((1,), (1,)), ((), ()))


def remote(src, dst, send, recv, where):
    return pltpu.make_async_remote_copy(
        src_ref=src,
        dst_ref=dst,
        send_sem=send,
        recv_sem=recv,
        device_id=where,
        device_id_type=MESH,
    )


def lane_marks(marks, count):
    return jnp.concatenate(
        [jnp.full((1, BS), marks(j), jnp.int32) for j in range(count)], axis=1
    ).astype(jnp.float32).astype(jnp.bfloat16)


def kernel(
    nrow,
    ncol,
    ainv,
    pattern,
    rows_a,
    rows_b,
    panel_a,
    panel_b,
    tri_a,
    tri_b,
    cross,
    weights,
    out,
    a_cat,
    pan,
    tri,
    full,
    mt,
    xt,
    gt,
    coupled,
    part,
    fromp,
    total,
    fromx,
    summed,
    rs,
    a_sem,
    pan_sem,
    tri_sem,
    g_send,
    g_recv,
    p_send,
    p_recv,
    x_send,
    x_recv,
    r_send,
    r_recv,
    in_sem,
):
    me_r, me_c, me_p = (lax.axis_index(name) for name in ("row", "col", "pole"))
    other = 1 - me_p
    tile_rows, tile_cols = ainv.shape[2], ainv.shape[3]
    width = tri_a.shape[2]
    share = tile_rows // ncol
    chunk = tile_rows // CHUNKS
    per_chunk = ncol // CHUNKS
    ring = nrow // 2
    nz = ncol // 2
    me_z, me_h = lax.div(me_c, 2), lax.rem(me_c, 2)
    per_z = nz // CHUNKS

    def col_at(z, h):
        return z * 2 + h

    marks = (rows_a, rows_b)

    pan_copies = [
        pltpu.make_async_copy(ref.at[0], pan.at[s], pan_sem.at[s])
        for s, ref in enumerate((panel_a, panel_b))
    ]
    tri_copies = [
        pltpu.make_async_copy(ref.at[0], tri.at[s], tri_sem.at[s])
        for s, ref in enumerate((tri_a, tri_b, cross))
    ]
    a_copies = [
        pltpu.make_async_copy(
            ainv.at[0, d], a_cat.at[:, d * tile_cols : (d + 1) * tile_cols], a_sem.at[d]
        )
        for d in range(2)
    ]
    for copy in pan_copies:
        copy.start()

    def row_at(step):
        dx, dy = step
        x, y = lax.div(me_r, ring), lax.rem(me_r, ring)
        return lax.rem(x + dx, 2) * ring + lax.rem(y + dy + ring, ring)

    barrier = pltpu.get_barrier_semaphore()
    row_partners = ((0, 1), (0, -1), (0, 2), (1, 0))
    for step in row_partners:
        pl.semaphore_signal(
            barrier, inc=1, device_id={"row": row_at(step)}, device_id_type=MESH
        )
    pl.semaphore_signal(barrier, inc=1, device_id={"pole": other}, device_id_type=MESH)

    pl.semaphore_signal(
        barrier, inc=1, device_id={"col": col_at(me_z, 1 - me_h)}, device_id_type=MESH
    )

    def along_z(step):
        return {"col": col_at(lax.rem(me_z + step + nz, nz), me_h)}

    for step in (1, -1):
        pl.semaphore_signal(barrier, inc=1, device_id=along_z(step), device_id_type=MESH)

    for copy in tri_copies + a_copies:
        copy.start()

    for s in range(2):
        pan_copies[s].wait()
        keep = lane_marks(lambda j: marks[s][j], tile_cols // BS)
        full[s, me_r] = pan[s] * keep[None]

    pl.semaphore_wait(barrier, len(row_partners) + 4)

    hops = ((((1,0),(0,0),None,None),((0,2),(0,0),None,None),((0,1),(0,0),None,None),((0,-1),(0,0),None,None),((0,1),(1,0),None,0),((0,-1),(1,0),None,0),((1,0),(0,2),None,1)), (((1,0),(0,0),None,None),((0,2),(0,0),None,None),((0,1),(0,0),None,None),((0,-1),(0,0),None,None),((0,1),(1,0),1,0),((0,-1),(1,0),0,0),((1,0),(0,-1),0,2),((1,0),(0,1),1,3),((1,0),(0,2),None,1)))

    def gather_copy(s, i):
        to, owner, part_of, _ = hops[s][i]
        block = full.at[s, row_at(owner)]
        if part_of is not None:
            block = block.at[part_of]
        return remote(block, block, g_send.at[s, i], g_recv.at[s, i], {"row": row_at(to)})

    arrived = set()

    def arrive(s, i):
        if (s, i) not in arrived:
            arrived.add((s, i))
            gather_copy(s, i).wait_recv()

    def pass_blocks(order):
        for s, i in order:
            if hops[s][i][3] is not None:
                arrive(s, hops[s][i][3])
            gather_copy(s, i).start()

    def tell(turn_of):
        for side, step in enumerate((1, -1)):
            pl.semaphore_signal(
                in_sem.at[turn_of, side],
                inc=1,
                device_id=along_z(step * (turn_of + 1)),
                device_id_type=MESH,
            )

    def hear(turn_of):
        for side in range(2):
            pl.semaphore_wait(in_sem.at[turn_of, side], 1)

    tell(0)
    pass_blocks(((0, 0), (0, 1), (1, 0), (1, 1), (0, 2), (0, 3), (1, 2), (1, 3)))

    w_re, w_im = weights[0, 0], weights[0, 1]

    def scale(s):
        tri_copies[s].wait()
        t_re, t_im = tri[s, 0].astype(jnp.float32), tri[s, 1].astype(jnp.float32)
        m_re = (w_im * t_im - w_re * t_re).T.astype(jnp.bfloat16)
        m_im = (-w_im * t_re - w_re * t_im).T.astype(jnp.bfloat16)
        mt[s, :width, :width] = m_im
        mt[s, :width, width:] = m_re
        mt[s, width:, :width] = m_re
        mt[s, width:, width:] = -m_im

    scale(0)

    pass_blocks(((0, 4), (0, 5), (0, 6), (1, 4), (1, 5), (1, 8), (1, 6), (1, 7)))

    hear(0)
    tell(1)
    for copy in a_copies:
        copy.wait()

    @pl.loop(0, tile_rows // BS)
    def _(b):
        rows = pl.ds(pl.multiple_of(b * BS, BS), BS)
        keep = lane_marks(lambda j: pattern[j, b], tile_cols // BS)
        for d in range(2):
            columns = slice(d * tile_cols, (d + 1) * tile_cols)
            a_cat[rows, columns] = a_cat[rows, columns] * keep

    def mul(a, b):
        return jnp.dot(a, b, preferred_element_type=jnp.float32)

    def couple():
        tri_copies[2].wait()
        x_re = mul(tri[2, 0], tri[1, 0]) - mul(tri[2, 1], tri[1, 1])
        x_im = mul(tri[2, 0], tri[1, 1]) + mul(tri[2, 1], tri[1, 0])
        x_re, x_im = x_re.T.astype(jnp.bfloat16), x_im.T.astype(jnp.bfloat16)
        xt[:width, :width] = -x_re
        xt[:width, width:] = -x_im
        xt[width:, :width] = x_im
        xt[width:, width:] = -x_re

    scale(1)
    couple()
    hear(1)

    def pole_copy(s, q):
        rows = pl.ds(pl.multiple_of(q * chunk, chunk), chunk)
        return remote(
            part.at[s, other, rows],
            fromp.at[s, rows],
            p_send.at[s, q],
            p_recv.at[s, q],
            {"pole": other},
        )

    def x_copy(s, q):
        shares = pl.ds(q * per_z, per_z)
        return remote(
            total.at[s, 1 - me_h, shares],
            fromx.at[s, shares],
            x_send.at[s, q],
            x_recv.at[s, q],
            {"col": col_at(me_z, 1 - me_h)},
        )

    def send_copy(s, to):
        return remote(
            summed.at[s, to],
            rs.at[s, me_z],
            r_send.at[s, to],
            r_recv.at[s, me_z],
            {"col": col_at(to, me_h)},
        )

    def take_copy(s, frm):
        return remote(
            summed.at[s, me_z],
            rs.at[s, frm],
            r_send.at[s, me_z],
            r_recv.at[s, frm],
            {"col": col_at(frm, me_h)},
        )

    first = lax.div(me_c, per_chunk)

    def turn(n):
        off = CHUNKS // 2 + lax.div(n + 1, 2) * (1 - 2 * lax.rem(n, 2))
        return lax.rem(first + off, CHUNKS)

    def pass_on(s):
        @pl.loop(0, CHUNKS)
        def _(n):
            q = turn(n)
            x_copy(s, q).wait_recv()
            shares = pl.ds(q * per_z, per_z)
            summed[s, shares] = (
                total[s, me_h, shares].astype(jnp.float32) + fromx[s, shares].astype(jnp.float32)
            ).astype(jnp.bfloat16)
            for j in range(per_z):
                to = q * per_z + j

                @pl.when(to != me_z)
                def _():
                    send_copy(s, to).start()

    for s in range(2):
        for i in range(len(hops[s])):
            arrive(s, i)

        for half in range(2):
            o_rows = slice(half * width, (half + 1) * width)
            lower = [full[s, :, d].reshape(width, tile_cols) for d in range(2)]
            g = mul(mt[s, o_rows, :width], lower[0]) + mul(mt[s, o_rows, width:], lower[1])
            if s == 1:
                g += coupled[half]
            gt[s, :, half * tile_cols : (half + 1) * tile_cols] = g.astype(jnp.bfloat16)

        @pl.loop(0, CHUNKS)
        def _(n):
            q = turn(n)
            rows = pl.ds(pl.multiple_of(q * chunk, chunk), chunk)
            c = lax.dot_general(
                a_cat[rows, :], gt[s], NT, preferred_element_type=jnp.float32
            ).astype(jnp.bfloat16)
            part[s, 0, rows] = c[:, :BS]
            part[s, 1, rows] = c[:, BS:]
            pole_copy(s, q).start()

        if s == 0:
            for half in range(2):
                o_rows = slice(half * width, (half + 1) * width)
                coupled[half] = mul(xt[o_rows, :width], gt[0, :, :tile_cols]) + mul(
                    xt[o_rows, width:], gt[0, :, tile_cols:]
                )

        @pl.loop(0, CHUNKS)
        def _(n):
            q = turn(n)
            rows = pl.ds(pl.multiple_of(q * chunk, chunk), chunk)
            pole_copy(s, q).wait_recv()
            both = part[s, me_p, rows].astype(jnp.float32) + fromp[s, rows].astype(jnp.float32)
            both = both.astype(jnp.bfloat16).reshape(per_z, 2, share, BS)
            for h in range(2):
                for j in range(per_z):
                    total[s, h, q * per_z + j] = both[j, h]
            x_copy(s, q).start()

    for s in range(2):
        pass_on(s)

    for s in range(2):
        for i in range(len(hops[s])):
            gather_copy(s, i).wait_send()

        @pl.loop(0, CHUNKS)
        def _(q):
            pole_copy(s, q).wait_send()
            x_copy(s, q).wait_send()

    for s in range(2):

        def add(i, acc):
            frm = lax.rem(me_z + i, nz)
            take_copy(s, frm).wait_recv()
            return acc + rs[s, frm].astype(jnp.float32)

        out[s] = lax.fori_loop(1, nz, add, summed[s, me_z].astype(jnp.float32))

    for s in range(2):

        @pl.loop(1, nz)
        def _(i):
            send_copy(s, lax.rem(me_z + i, nz)).wait_send()


def solution(mesh):
    nrow, ncol = mesh.shape["row"], mesh.shape["col"]

    def per_device(
        ainv, pattern, rows_a, rows_b, panel_a, panel_b, tri_a, tri_b, cross_b, weights
    ):
        tile_rows, tile_cols = ainv.shape[2:]
        width, own_width = tri_a.shape[2], panel_a.shape[2]
        share = tile_rows // ncol
        anywhere = pl.BlockSpec(memory_space=pl.ANY)
        scalars = pl.BlockSpec(memory_space=pltpu.SMEM)
        whole = pl.BlockSpec(memory_space=pltpu.VMEM)
        bf16 = jnp.bfloat16
        dma = pltpu.SemaphoreType.DMA
        dens = pl.pallas_call(
            functools.partial(kernel, nrow, ncol),
            out_shape=pltpu.VMEM((2, share, BS), jnp.float32),
            in_specs=[anywhere] + [scalars] * 3 + [anywhere] * 5 + [scalars],
            out_specs=whole,
            scratch_shapes=[
                pltpu.VMEM((tile_rows, 2 * tile_cols), bf16),
                pltpu.VMEM((2, 2, own_width, tile_cols), bf16),
                pltpu.VMEM((3, 2, width, width), bf16),
                pltpu.VMEM((2, nrow, 2, own_width, tile_cols), bf16),
                pltpu.VMEM((2, 2 * width, 2 * width), bf16),
                pltpu.VMEM((2 * width, 2 * width), bf16),
                pltpu.VMEM((2, width, 2 * tile_cols), bf16),
                pltpu.VMEM((2, width, tile_cols), jnp.float32),
                pltpu.VMEM((2, 2, tile_rows, BS), bf16),
                pltpu.VMEM((2, tile_rows, BS), bf16),
                pltpu.VMEM((2, 2, ncol // 2, share, BS), bf16),
                pltpu.VMEM((2, ncol // 2, share, BS), bf16),
                pltpu.VMEM((2, ncol // 2, share, BS), bf16),
                pltpu.VMEM((2, ncol // 2, share, BS), bf16),
                dma((2,)),
                dma((2,)),
                dma((3,)),
                dma((2, 10)),
                dma((2, 10)),
                dma((2, CHUNKS)),
                dma((2, CHUNKS)),
                dma((2, CHUNKS)),
                dma((2, CHUNKS)),
                dma((2, ncol // 2)),
                dma((2, ncol // 2)),
                pltpu.SemaphoreType.REGULAR((2, 2)),
            ],
            compiler_params=pltpu.CompilerParams(
                collective_id=0, has_side_effects=True, vmem_limit_bytes=56 << 20
            ),
        )(ainv, pattern.T, rows_a, rows_b, panel_a, panel_b, tri_a, tri_b, cross_b, weights)
        return dens[0], dens[1]

    placed = (
        P("pole", None, "row", "col"),
        P("row", "col"),
        P("col"),
        P("col"),
        P("pole", None, "row", "col"),
        P("pole", None, "row", "col"),
        P("pole", None, None, None),
        P("pole", None, None, None),
        P("pole", None, None, None),
        P("pole", None),
    )
    return jax.shard_map(
        per_device,
        mesh=mesh,
        in_specs=placed,
        out_specs=(P(("row", "col"), "pole"), P(("row", "col"), "pole")),
        check_vma=False,
    )
```
